256 devices in a mesh: gx: 16 (over y, x), gy: 16 (over z, core).
Axes of the slice: x: 4, y: 4, z: 8, core: 2. Of those that a mesh axis runs over, the one named last changes fastest.
Arguments:
- amplitudes: bfloat16 [6, 16, 2048, 2048], P(None, 'gy', 'gx'), may hold values from -6 to 6
- coulomb: bfloat16 [16, 2048, 1, 2048], P('gy', 'gx'), may hold values from -0.03125 to 0.03125
- exchange_ints: bfloat16 [16, 2048, 1, 2048], P('gy', 'gx'), may hold values from -0.03125 to 0.03125
- block_sizes: int32 [4], replicated, may hold values from 64 to 1024, as said below
- occ_irreps: int32 [250], replicated, may hold values from 0 to 3
- tile_i: int32 [6], replicated, may hold values from 0 to 249
- tile_j: int32 [1], replicated, may hold values from 0 to 249
Outputs:
- residual: float32 [6, 2048, 1, 2048], P(None, 'gx', None, 'gy')
The draws below stay inside these ranges and needn't reach their ends.
Inputs may be any that keep to these rules, and one draw needn't show every extreme that they name: `block_sizes`: the sizes sum to 2048; one irrep has exactly 64, and one has exactly half of 2048, rounded down.
All inputs are finite; a program needn't handle non-finite values.
Results may differ from the reference program's by a relative error of at most 0.0003.
Values may be sent and summed in bfloat16 or wider, within the bound.
A program may use at most 128 MiB of HBM per device.

```python
import jax
import jax.numpy as jnp
from jax import lax

V = 2048
O = 250
NIRREP = 4
BLOCK_MIN = 64
NI = 6
NJ = 1
NK = 16


def draw_block_sizes(key, part):
    key = jax.random.fold_in(key, 11)
    largest = V // 2
    remaining = V - largest - BLOCK_MIN
    cut_key, order_key = jax.random.split(key, 2)
    cut = jax.random.randint(cut_key, (), BLOCK_MIN, remaining - BLOCK_MIN + 1)
    ordered = jnp.stack([jnp.int32(BLOCK_MIN), jnp.int32(largest), cut.astype(jnp.int32), (remaining - cut).astype(jnp.int32)]).astype(jnp.int32)
    placing = jax.random.permutation(order_key, NIRREP)
    return jnp.zeros((NIRREP,), jnp.int32).at[placing].set(ordered)


def with_ends(array, own_key, low, high):
    longest = array.shape.index(max(array.shape))
    spots = []
    for shift in (0, 1):
        where = [jax.random.randint(jax.random.fold_in(own_key, axis), (), 0, length) for axis, length in enumerate(array.shape)]
        where[longest] = (where[longest] + shift) % array.shape[longest]
        spots.append(tuple(where))
    return array.at[spots[0]].set(low).at[spots[1]].set(high)


def shard_levels(rng, shape, shards, smallest, top_value):
    def one(dim, blocks):
        steps = jax.random.uniform(jax.random.fold_in(jax.random.fold_in(rng, 6), dim), (blocks,), jnp.float32, smallest / len(shards), top_value / len(shards))
        return jnp.repeat(jnp.exp(steps), shape[dim] // blocks).reshape((-1,) + (1,) * (len(shape) - dim - 1))

    gain = one(*shards[0])
    for cut in shards[1:]:
        gain = gain * one(*cut)
    return gain


def normal_values(key, shape, spread, reach, pieces=(), held_as=jnp.bfloat16):
    entries = jax.random.normal(key, shape, jnp.float32) * spread
    if len(pieces) > 0:
        entries = shard_levels(key, shape, pieces, -0.22, 0.18) * entries
    return jnp.clip(entries, min=-reach, max=reach).astype(held_as)


def setup_inputs(seed: int = 0) -> dict:
    arg_keys = jax.random.split(jax.random.key(seed), 8)
    amplitudes = normal_values(arg_keys[0], (NI, NK, V, V), 1.0, 6.0, ((1, 16), (2, 16)))
    coulomb = normal_values(arg_keys[1], (NK, V, NJ, V), (NK * V) ** -0.5, 0.03125, ((0, 16), (1, 16)))
    exchange_ints = normal_values(arg_keys[2], (NK, V, NJ, V), (NK * V) ** -0.5, 0.03125, ((0, 16), (1, 16)))
    block_sizes = draw_block_sizes(jax.random.fold_in(arg_keys[7], 71), 0)
    occ_irreps = with_ends(jax.random.randint(arg_keys[4], (O,), 0, NIRREP), jax.random.fold_in(arg_keys[4], 1), 0, NIRREP - 1).astype(jnp.int32)
    tile_i = with_ends(jax.random.randint(arg_keys[5], (NI,), 0, O), jax.random.fold_in(arg_keys[5], 1), 0, O - 1).astype(jnp.int32)
    tile_j = jax.random.randint(arg_keys[6], (NJ,), 0, O).astype(jnp.int32)
    return dict(amplitudes=amplitudes, coulomb=coulomb, exchange_ints=exchange_ints, block_sizes=block_sizes, occ_irreps=occ_irreps, tile_i=tile_i, tile_j=tile_j)


def irrep_of(index, block_sizes):
    block_ends = jnp.cumsum(block_sizes.astype(jnp.int32)).astype(jnp.int32)
    return jnp.sum((index[:, None] >= block_ends[None, :-1]).astype(jnp.int32), axis=1).astype(jnp.int32)


def occupied_irrep(tile_ids, occ_irreps):
    orbitals = jnp.arange(occ_irreps.shape[0], dtype=jnp.int32)
    onehot = (tile_ids[:, None] == orbitals[None, :]).astype(jnp.int32)
    return jnp.sum(onehot * occ_irreps[None, :], axis=1).astype(jnp.int32)


def reference(amplitudes, coulomb, exchange_ints, block_sizes, occ_irreps, tile_i, tile_j):
    ni_count = amplitudes.shape[0]
    virt = amplitudes.shape[2]
    nj_count = coulomb.shape[2]

    def step_k(total, inputs):
        amp_k, coul_k, exch_k = inputs
        left = amp_k.reshape(ni_count * virt, virt)
        swap_k = jnp.swapaxes(amp_k, 1, 2).reshape(ni_count * virt, virt)
        first = jnp.dot(left, coul_k.reshape(virt, nj_count * virt), preferred_element_type=jnp.float32)
        second = jnp.dot(swap_k, exch_k.reshape(virt, nj_count * virt), preferred_element_type=jnp.float32)
        return total + 2.0 * first - second, None

    start_total = jnp.zeros((ni_count * virt, nj_count * virt), jnp.float32)
    cycle, _ = lax.scan(step_k, start_total, (jnp.swapaxes(amplitudes, 0, 1), coulomb, exchange_ints))
    cycle = cycle.reshape(ni_count, virt, nj_count, virt)
    virt_irrep = irrep_of(jnp.arange(virt, dtype=jnp.int32), block_sizes)
    pair_irrep = jnp.bitwise_xor(occupied_irrep(tile_i, occ_irreps)[:, None], occupied_irrep(tile_j, occ_irreps)[None, :])
    allowed = jnp.bitwise_xor(virt_irrep[None, :, None, None], virt_irrep[None, None, None, :]) == pair_irrep[:, None, :, None]
    return jnp.where(allowed, cycle, jnp.float32(0.0))
```

```python
import jax
import jax.numpy as jnp
from jax import lax
from jax.experimental import pallas as pl
from jax.experimental.pallas import tpu as pltpu
from jax.sharding import PartitionSpec as P

MESH = pl.DeviceIdType.MESH
NY, NX, NZ = 4, 4, 8
NIRREP = 4
NS = 3
BLK = 128
GRP = NY * BLK
TILE = 256
SUB = 8
ROWS = GRP // SUB
WIN = 33
LAST = ROWS - WIN
TOP = 17
F32 = jnp.float32


def step_tile(step):
    half = lax.div(step + 1, 2)
    return 4 + half * (1 - 2 * lax.rem(step, 2))


def kernel(amp, coul, exch, sizes, occ, tile_i, tile_j, out, left, raw, right, dense, part, zin, wide, yout, yin,
           t1_recv, t2_recv, t_send, w_recv, w_send, c_recv, c_send, z_recv, z_send, y_recv, y_send):
    gx, gy = lax.axis_index("gx"), lax.axis_index("gy")
    y, x = lax.div(gx, NX), lax.rem(gx, NX)
    z, core = lax.div(gy, 2), lax.rem(gy, 2)

    def device(dy=0, dx=0, dz=0, dc=0):
        y2, x2 = lax.rem(y + dy, NY), lax.rem(x + dx, NX)
        z2, core2 = lax.rem(z + dz, NZ), lax.rem(core + dc, 2)
        return (y2 * NX + x2, z2 * 2 + core2)

    barrier = pltpu.get_barrier_semaphore()
    partners = [dict(dy=dy, dc=dc) for dy in range(NY) for dc in range(2) if dy or dc]
    partners += [dict(dx=dx, dc=dc) for dx in range(1, NX) for dc in range(2)]
    partners += [dict(dz=1), dict(dz=NZ - 1)]
    for partner in partners:
        pl.semaphore_signal(barrier, inc=1, device_id=device(**partner), device_id_type=MESH)
    pl.semaphore_wait(barrier, len(partners))

    def loop(count, body, unroll=None):
        lax.fori_loop(0, count, lambda n, carry: (body(n), carry)[1], 0, unroll=unroll)

    def send_amplitudes(s):
        for dc in range(2):
            row = 3 * lax.rem(core + dc, 2) + s
            for dy in range(NY):
                y2 = lax.rem(y + dy, NY)
                src = amp.at[row, :, pl.ds(pl.multiple_of(GRP * y2, GRP), GRP)]
                dst = left.at[s, pl.ds(pl.multiple_of(BLK * y, BLK), BLK), pl.ds(pl.multiple_of(GRP * core, GRP), GRP)]
                if dy or dc:
                    pltpu.make_async_remote_copy(
                        src, dst, t_send.at[s], t1_recv.at[s], device_id=device(dy=dy, dc=dc), device_id_type=MESH
                    ).start()
                else:
                    pltpu.make_async_copy(src, dst, t1_recv.at[s]).start()
            for dx in range(NX):
                x2 = lax.rem(x + dx, NX)
                for y2 in range(NY):
                    src = amp.at[row, :, pl.ds(pl.multiple_of(GRP * y2 + BLK * x2, BLK), BLK)]
                    dst = raw.at[s, core, pl.ds(pl.multiple_of(BLK * x, BLK), BLK), pl.ds(BLK * y2, BLK)]
                    if dx or dc:
                        pltpu.make_async_remote_copy(
                            src, dst, t_send.at[s], t2_recv.at[s], device_id=device(dx=dx, dc=dc), device_id_type=MESH
                        ).start()
                    else:
                        pltpu.make_async_copy(src, dst, t2_recv.at[s]).start()

    def send_integrals(step):
        tile = lax.rem(z + step_tile(step), NZ)
        columns = pl.ds(pl.multiple_of(TILE * tile, TILE), TILE)
        for dx in range(NX):
            for term, ref in ((0, coul), (1, exch)):
                src, dst = ref.at[:, columns], right.at[step, term, core, x]
                if dx:
                    pltpu.make_async_remote_copy(
                        src, dst, w_send.at[step], w_recv.at[step], device_id=device(dx=dx), device_id_type=MESH
                    ).start()
                else:
                    pltpu.make_async_copy(src, dst, w_recv.at[step]).start()

    def wait_bytes(ref, sem):
        pltpu.make_async_copy(ref, ref, sem).wait()

    def take_amplitudes(s):
        wait_bytes(left.at[s, :, pl.ds(0, 2 * GRP)], t1_recv.at[s])
        wait_bytes(raw.at[s], t2_recv.at[s])
        for k in range(2):
            left[s, :, pl.ds((2 + k) * GRP, GRP)] = (raw[s, k] * jnp.asarray(-0.5, jnp.bfloat16)).T

    def share_integrals(step):
        return pltpu.make_async_remote_copy(
            right.at[step, :, core], right.at[step, :, core], c_send.at[step], c_recv.at[step],
            device_id=device(dc=1), device_id_type=MESH,
        )

    def take_integrals(step):
        wait_bytes(right.at[step, :, core], w_recv.at[step])
        share_integrals(step).start()
        wait_bytes(right.at[step, :, 1 - core], c_recv.at[step])

    first_end = sizes[0]
    second_end = first_end + sizes[1]
    third_end = second_end + sizes[2]

    def irrep(index):
        return (
            (index >= first_end).astype(jnp.int32)
            + (index >= second_end).astype(jnp.int32)
            + (index >= third_end).astype(jnp.int32)
        )

    def pair_irrep(i):
        return occ[tile_i[i]] ^ occ[tile_j[0]]

    def window(i, col_irrep):
        row_irrep = pair_irrep(i) ^ col_irrep
        begin = jnp.where(row_irrep > 0, sizes[0], 0) + jnp.where(row_irrep > 1, sizes[1], 0)
        begin = begin + jnp.where(row_irrep > 2, sizes[2], 0)
        block = lax.div(begin, GRP)
        local = block * BLK + jnp.clip(begin - block * GRP - BLK * x, 0, BLK)
        return jnp.minimum(lax.div(local, SUB), LAST)

    def columns_irrep(step):
        tile = lax.rem(z + step_tile(step), NZ)
        return irrep(TILE * tile + lax.broadcasted_iota(jnp.int32, (1, TILE), 1))

    def z_copy(s, step):
        up = lax.rem(step, 2)
        return pltpu.make_async_remote_copy(
            part.at[s, step], zin.at[s, step + 2], z_send.at[s, step], z_recv.at[s, step + 2],
            device_id=device(dz=up + (1 - up) * (NZ - 1)), device_id_type=MESH,
        )

    def z_first(s):
        upper, lower = pl.ds(0, TOP), pl.ds(TOP, WIN - TOP)
        return [
            pltpu.make_async_remote_copy(
                part.at[s, 0, upper], zin.at[s, 1, upper], z_send.at[s, 0], z_recv.at[s, 1],
                device_id=device(dz=1), device_id_type=MESH,
            ),
            pltpu.make_async_remote_copy(
                part.at[s, 0, lower], zin.at[s, 2, lower], z_send.at[s, 7], z_recv.at[s, 2],
                device_id=device(dz=NZ - 1), device_id_type=MESH,
            ),
        ]

    def y_copy(s, dy, dc):
        y2, core2 = lax.rem(y + dy, NY), lax.rem(core + dc, 2)
        src, dst = yout.at[s, 2 * y2 + core2], yin.at[3 * core + s, y]
        if dy or dc:
            return pltpu.make_async_remote_copy(
                src, dst, y_send.at[s], y_recv.at[3 * core + s], device_id=device(dy=dy, dc=dc), device_id_type=MESH
            )
        return pltpu.make_async_copy(src, dst, y_recv.at[3 * core + s])

    def compute(s, step):
        product = jnp.dot(left[s], right[step].reshape(4 * GRP, TILE), preferred_element_type=F32)
        dense[...] = product.reshape(ROWS, SUB, TILE)
        kinds = columns_irrep(step)
        begins = [window(3 * core + s, kind) for kind in range(NIRREP)]

        def pack(row):
            packed = dense[begins[0] + row]
            for kind in range(1, NIRREP):
                packed = jnp.where(kinds == kind, dense[begins[kind] + row], packed)
            part[s, step, row] = packed

        loop(WIN, pack, unroll=True)

    def pass_on(s, step):
        @pl.when(step == 0)
        def _():
            for copy in z_first(s):
                copy.start()

        @pl.when(step == 1)
        def _():
            rows = pl.ds(0, TOP)
            wait_bytes(zin.at[s, 1, rows], z_recv.at[s, 1])
            part[s, 1, rows] += zin[s, 1, rows]

        @pl.when(step == 2)
        def _():
            rows = pl.ds(TOP, WIN - TOP)
            wait_bytes(zin.at[s, 2, rows], z_recv.at[s, 2])
            part[s, 2, rows] += zin[s, 2, rows]

        @pl.when((step > 2) & (step < 7))
        def _():
            wait_bytes(zin.at[s, step], z_recv.at[s, step])
            part[s, step] += zin[s, step]

        @pl.when((step > 0) & (step < 7))
        def _():
            z_copy(s, step).start()

    def finish(s):
        wait_bytes(zin.at[s, 7], z_recv.at[s, 7])
        wait_bytes(zin.at[s, 8], z_recv.at[s, 8])
        wide[pl.ds(LAST, WIN)] = part[s, 7] + zin[s, 7] + zin[s, 8]
        kinds = columns_irrep(7)
        begins = [LAST - window(3 * core + s, kind) for kind in range(NIRREP)]
        for block in range(NY):

            def unpack(row):
                rows = wide[begins[0] + block * (BLK // SUB) + row]
                for kind in range(1, NIRREP):
                    rows = jnp.where(kinds == kind, wide[begins[kind] + block * (BLK // SUB) + row], rows)
                for half in range(2):
                    yout[s, 2 * block + half, row] = rows[:, half * BLK:(half + 1) * BLK]

            loop(BLK // SUB, unpack, unroll=True)
        for dc in range(2):
            for dy in range(NY):
                y_copy(s, dy, dc).start()

    def write(i):
        wait_bytes(yin.at[i], y_recv.at[i])
        total = 2.0 * (yin[i, 0] + yin[i, 1] + yin[i, 2] + yin[i, 3]).reshape(BLK, BLK)
        rows = irrep(BLK * gx + lax.broadcasted_iota(jnp.int32, (BLK, 1), 0))
        columns = irrep(BLK * gy + lax.broadcasted_iota(jnp.int32, (1, BLK), 1))
        out[i] = jnp.where((rows ^ columns) == pair_irrep(i), total, 0.0)

    loop(NS, send_amplitudes)
    loop(NZ, send_integrals)
    wide[pl.ds(0, LAST)] = jnp.zeros((LAST, SUB, TILE), F32)
    wide[pl.ds(ROWS, LAST)] = jnp.zeros((LAST, SUB, TILE), F32)
    loop(NS, take_amplitudes)

    def one(n):
        step, s = lax.div(n, NS), lax.rem(n, NS)

        @pl.when(s == 0)
        def _():
            take_integrals(step)

        compute(s, step)
        pass_on(s, step)

    loop(NZ * NS, one)
    loop(NS, finish)
    loop(2 * NS, lambda n: write(3 * lax.rem(n, 2) + lax.div(n, 2)))

    def drain(s):
        wait_bytes(left.at[s, pl.ds(0, 448), :], t_send.at[s])
        for copy in z_first(s):
            copy.wait_send()
        loop(6, lambda step: z_copy(s, step + 1).wait_send())
        wait_bytes(yout.at[s, pl.ds(0, 7)], y_send.at[s])

    loop(NS, drain)

    def drain_integrals(step):
        wait_bytes(right.at[step, 0, :, pl.ds(0, 3)], w_send.at[step])
        share_integrals(step).wait_send()

    loop(NZ, drain_integrals)


def per_device(amplitudes, coulomb, exchange_ints, block_sizes, occ_irreps, tile_i, tile_j):
    depth, columns = coulomb.shape[1], coulomb.shape[3]
    count = amplitudes.shape[0]
    anywhere, scalars = pl.BlockSpec(memory_space=pl.ANY), pl.BlockSpec(memory_space=pltpu.SMEM)
    dma = pltpu.SemaphoreType.DMA
    residual = pl.pallas_call(
        kernel,
        out_shape=jax.ShapeDtypeStruct((count, BLK, BLK), F32),
        in_specs=[anywhere] * 3 + [scalars] * 4,
        out_specs=pl.BlockSpec(memory_space=pltpu.VMEM),
        scratch_shapes=[
            pltpu.VMEM((NS, GRP, 4 * GRP), jnp.bfloat16),
            pltpu.VMEM((NS, 2, GRP, GRP), jnp.bfloat16),
            pltpu.VMEM((NZ, 2, 2, NX, BLK, TILE), jnp.bfloat16),
            pltpu.VMEM((ROWS, SUB, TILE), F32),
            pltpu.VMEM((NS, NZ, WIN, SUB, TILE), F32),
            pltpu.VMEM((NS, NZ + 1, WIN, SUB, TILE), F32),
            pltpu.VMEM((ROWS + LAST, SUB, TILE), F32),
            pltpu.VMEM((NS, 2 * NY, BLK // SUB, SUB, BLK), F32),
            pltpu.VMEM((2 * NS, NY, BLK // SUB, SUB, BLK), F32),
            dma((NS,)), dma((NS,)), dma((NS,)),
            dma((NZ,)), dma((NZ,)), dma((NZ,)), dma((NZ,)),
            dma((NS, NZ + 1)), dma((NS, NZ)),
            dma((2 * NS,)), dma((NS,)),
        ],
        compiler_params=pltpu.CompilerParams(
            collective_id=0, has_side_effects=True, vmem_limit_bytes=56 * 1024 * 1024
        ),
        cost_estimate=pl.CostEstimate(flops=12900000000, bytes_accessed=5000000, transcendentals=0),
    )(
        amplitudes.reshape(count, BLK, columns),
        coulomb.reshape(depth, columns),
        exchange_ints.reshape(depth, columns),
        block_sizes, occ_irreps, tile_i, tile_j,
    )
    return residual.reshape(count, BLK, 1, BLK)


def solution(mesh):
    return jax.shard_map(
        per_device,
        mesh=mesh,
        in_specs=(
            P(None, "gy", "gx", None),
            P("gy", "gx", None, None),
            P("gy", "gx", None, None),
            P(),
            P(),
            P(),
            P(),
        ),
        out_specs=P(None, "gx", None, "gy"),
        check_vma=False,
    )
```

```python
import jax
import jax.numpy as jnp
from jax import lax
from jax.experimental import pallas as pl
from jax.experimental.pallas import tpu as pltpu
from jax.sharding import PartitionSpec as P

MESH = pl.DeviceIdType.MESH
NY, NX, NZ = 4, 4, 8
NIRREP = 4
NS = 3
BLK = 128
GRP = NY * BLK
TILE = 256
SUB = 8
ROWS = GRP // SUB
WIN = 33
LAST = ROWS - WIN
SHARE, QUARTER = 8, 9
UPPER, LOWER = pl.ds(0, 17), pl.ds(17, 16)
Q_UPPER, Q_LOWER = pl.ds(0, 5), pl.ds(5, 4)
F32 = jnp.float32


def make_plan():
    units = sorted(
        [(s, step) for s in range(NS) for step in range(NZ)], key=lambda unit: ((unit[1] + 1) // 2, unit[0], unit[1])
    )
    before = [("amp", s) for s in range(NS)] + [("own", step) for step in range(NZ)]
    early = [[] for _ in units]
    for s in range(NS):
        early[units.index((s, 0))] += [("got", s)]
    for step in range(NZ):
        early[units.index((0, step))] += [("share", step), ("have", step)]
    after = [("finish", 0), ("finish", 1)]
    for step in range(NZ):
        place = units.index((NS - 1, step)) + 6
        (early[place] if place < len(units) else after).append(("quarter", step))
    return units, before, early, after


UNITS, BEFORE, EARLY, AFTER = make_plan()


def step_tile(step):
    half = lax.div(step + 1, 2)
    return 4 + half * (1 - 2 * lax.rem(step, 2))


def kernel(amp, coul, exch, sizes, occ, tile_i, tile_j, out, left, raw, right, dense, part, zin, wide, yout, yin,
           split, quarter, qin, gout, gin, narrow, flat,
           t1_recv, t2_recv, t_send, w_recv, w_send, c_recv, c_send, z_recv, z_send, y_recv, y_send,
           s_recv, s_send, q_recv, q_send, g_recv, g_send):
    gx, gy = lax.axis_index("gx"), lax.axis_index("gy")
    y, x = lax.div(gx, NX), lax.rem(gx, NX)
    z, core = lax.div(gy, 2), lax.rem(gy, 2)

    def device(dy=0, dx=0, dz=0, dc=0):
        y2, x2 = lax.rem(y + dy, NY), lax.rem(x + dx, NX)
        z2, core2 = lax.rem(z + dz, NZ), lax.rem(core + dc, 2)
        return (y2 * NX + x2, z2 * 2 + core2)

    barrier = pltpu.get_barrier_semaphore()
    partners = [dict(dy=dy, dc=dc) for dy in range(NY) for dc in range(2) if dy or dc]
    partners += [dict(dx=dx, dc=dc) for dx in range(1, NX) for dc in range(2)]
    partners += [dict(dz=1), dict(dz=NZ - 1)]
    for partner in partners:
        pl.semaphore_signal(barrier, inc=1, device_id=device(**partner), device_id_type=MESH)
    pl.semaphore_wait(barrier, len(partners))

    def loop(count, body, unroll=None):
        lax.fori_loop(0, count, lambda n, carry: (body(n), carry)[1], 0, unroll=unroll)

    def send_amplitudes(s):
        for dc in range(2):
            row = 3 * lax.rem(core + dc, 2) + s
            for dy in range(NY):
                y2 = lax.rem(y + dy, NY)
                src = amp.at[row, :, pl.ds(pl.multiple_of(GRP * y2, GRP), GRP)]
                dst = left.at[s, pl.ds(pl.multiple_of(BLK * y, BLK), BLK), pl.ds(pl.multiple_of(GRP * core, GRP), GRP)]
                if dy or dc:
                    pltpu.make_async_remote_copy(
                        src, dst, t_send.at[s], t1_recv.at[s], device_id=device(dy=dy, dc=dc), device_id_type=MESH
                    ).start()
                else:
                    pltpu.make_async_copy(src, dst, t1_recv.at[s]).start()
            for dx in range(NX):
                x2 = lax.rem(x + dx, NX)
                for y2 in range(NY):
                    src = amp.at[row, :, pl.ds(pl.multiple_of(GRP * y2 + BLK * x2, BLK), BLK)]
                    dst = raw.at[s, core, pl.ds(pl.multiple_of(BLK * x, BLK), BLK), pl.ds(BLK * y2, BLK)]
                    if dx or dc:
                        pltpu.make_async_remote_copy(
                            src, dst, t_send.at[s], t2_recv.at[s], device_id=device(dx=dx, dc=dc), device_id_type=MESH
                        ).start()
                    else:
                        pltpu.make_async_copy(src, dst, t2_recv.at[s]).start()

    def send_integrals(step):
        tile = lax.rem(z + step_tile(step), NZ)
        columns = pl.ds(pl.multiple_of(TILE * tile, TILE), TILE)
        for dx in (1, 3, 2, 0):
            for term, ref in ((0, coul), (1, exch)):
                src, dst = ref.at[:, columns], right.at[step, term, core, x]
                if dx:
                    pltpu.make_async_remote_copy(
                        src, dst, w_send.at[step], w_recv.at[step], device_id=device(dx=dx), device_id_type=MESH
                    ).start()
                else:
                    pltpu.make_async_copy(src, dst, w_recv.at[step]).start()

    def wait_bytes(ref, sem):
        pltpu.make_async_copy(ref, ref, sem).wait()

    def take_amplitudes(s):
        wait_bytes(left.at[s, :, pl.ds(0, 2 * GRP)], t1_recv.at[s])
        wait_bytes(raw.at[s], t2_recv.at[s])
        for k in range(2):
            left[s, :, pl.ds((2 + k) * GRP, GRP)] = (raw[s, k] * jnp.asarray(-0.5, jnp.bfloat16)).T

    def share_integrals(step):
        return pltpu.make_async_remote_copy(
            right.at[step, :, core], right.at[step, :, core], c_send.at[step], c_recv.at[step],
            device_id=device(dc=1), device_id_type=MESH,
        )

    def take_integrals(step):
        wait_bytes(right.at[step, :, core], w_recv.at[step])
        share_integrals(step).start()

    def take_shared(step):
        wait_bytes(right.at[step, :, 1 - core], c_recv.at[step])

    first_end = sizes[0]
    second_end = first_end + sizes[1]
    third_end = second_end + sizes[2]

    def irrep(index):
        return (
            (index >= first_end).astype(jnp.int32)
            + (index >= second_end).astype(jnp.int32)
            + (index >= third_end).astype(jnp.int32)
        )

    def pair_irrep(i):
        return occ[tile_i[i]] ^ occ[tile_j[0]]

    def window(i, col_irrep):
        row_irrep = pair_irrep(i) ^ col_irrep
        begin = jnp.where(row_irrep > 0, sizes[0], 0) + jnp.where(row_irrep > 1, sizes[1], 0)
        begin = begin + jnp.where(row_irrep > 2, sizes[2], 0)
        block = lax.div(begin, GRP)
        local = block * BLK + jnp.clip(begin - block * GRP - BLK * x, 0, BLK)
        return jnp.minimum(lax.div(local, SUB), LAST)

    def columns_irrep(step):
        tile = lax.rem(z + step_tile(step), NZ)
        return irrep(TILE * tile + lax.broadcasted_iota(jnp.int32, (1, TILE), 1))

    def z_copy(s, step):
        up = lax.rem(step, 2)
        return pltpu.make_async_remote_copy(
            part.at[s, step], zin.at[s, step + 2], z_send.at[s, step], z_recv.at[s, step + 2],
            device_id=device(dz=up + (1 - up) * (NZ - 1)), device_id_type=MESH,
        )

    def z_first(s):
        return [
            pltpu.make_async_remote_copy(
                part.at[s, 0, rows], zin.at[s, slot, rows], z_send.at[s, sem], z_recv.at[s, slot],
                device_id=device(dz=dz), device_id_type=MESH,
            )
            for rows, slot, sem, dz in ((UPPER, 1, 0, 1), (LOWER, 2, 7, NZ - 1))
        ]

    def q_copy(step):
        up = lax.rem(step, 2)
        return pltpu.make_async_remote_copy(
            quarter.at[step], qin.at[step + 2], q_send.at[step], q_recv.at[step + 2],
            device_id=device(dz=up + (1 - up) * (NZ - 1)), device_id_type=MESH,
        )

    def q_first():
        return [
            pltpu.make_async_remote_copy(
                quarter.at[0, rows], qin.at[slot, rows], q_send.at[sem], q_recv.at[slot],
                device_id=device(dz=dz), device_id_type=MESH,
            )
            for rows, slot, sem, dz in ((Q_UPPER, 1, 0, 1), (Q_LOWER, 2, 7, NZ - 1))
        ]

    def split_rows(step):
        for dy in (1, 3, 2):
            y2 = lax.rem(y + dy, NY)
            pltpu.make_async_remote_copy(
                part.at[NS - 1, step, pl.ds(SHARE * y2, QUARTER)], split.at[step, y], s_send.at[step], s_recv.at[step],
                device_id=device(dy=dy), device_id_type=MESH,
            ).start()

    def g_copy(dy, dc):
        core2 = lax.rem(core + dc, 2)
        src, dst = gout.at[core2], gin.at[NY * core + y]
        if dy or dc:
            return pltpu.make_async_remote_copy(
                src, dst, g_send, g_recv.at[core], device_id=device(dy=dy, dc=dc), device_id_type=MESH
            )
        return pltpu.make_async_copy(src, dst, g_recv.at[core])

    def y_copy(s, dy, dc):
        y2, core2 = lax.rem(y + dy, NY), lax.rem(core + dc, 2)
        src, dst = yout.at[s, 2 * y2 + core2], yin.at[3 * core + s, y]
        if dy or dc:
            return pltpu.make_async_remote_copy(
                src, dst, y_send.at[s], y_recv.at[3 * core + s], device_id=device(dy=dy, dc=dc), device_id_type=MESH
            )
        return pltpu.make_async_copy(src, dst, y_recv.at[3 * core + s])

    def compute(s, step):
        product = jnp.dot(left[s], right[step].reshape(4 * GRP, TILE), preferred_element_type=F32)
        dense[...] = product.reshape(ROWS, SUB, TILE)
        kinds = columns_irrep(step)
        begins = [window(3 * core + s, kind) for kind in range(NIRREP)]

        def pack(row):
            packed = dense[begins[0] + row]
            for kind in range(1, NIRREP):
                packed = jnp.where(kinds == kind, dense[begins[kind] + row], packed)
            part[s, step, row] = packed

        loop(WIN, pack, unroll=True)

    def pass_on(s, step):
        @pl.when(step == 0)
        def _():
            for copy in z_first(s):
                copy.start()

        for place, rows in ((1, UPPER), (2, LOWER)):

            @pl.when(step == place)
            def _():
                wait_bytes(zin.at[s, place, rows], z_recv.at[s, place])
                part[s, place, rows] += zin[s, place, rows]

        @pl.when((step > 2) & (step < 7))
        def _():
            wait_bytes(zin.at[s, step], z_recv.at[s, step])
            part[s, step] += zin[s, step]

        @pl.when((step > 0) & (step < 7))
        def _():
            z_copy(s, step).start()

    def pass_quarter(step):
        wait_bytes(split.at[step, pl.ds(0, NY - 1)], s_recv.at[step])
        total = part[NS - 1, step, pl.ds(SHARE * y, QUARTER)]
        for dy in range(1, NY):
            total = total + split[step, lax.rem(y + dy, NY)]
        quarter[step] = total
        if step == 0:
            for copy in q_first():
                copy.start()
            return
        for slot in (7, 8) if step == 7 else (step,):
            rows = {1: Q_UPPER, 2: Q_LOWER}.get(slot, pl.ds(0, QUARTER))
            wait_bytes(qin.at[slot, rows], q_recv.at[slot])
            quarter[step, rows] += qin[slot, rows]
        if step < 7:
            q_copy(step).start()
            return
        for half in range(2):
            gout[half] = quarter[7, :, :, pl.ds(half * BLK, BLK)]
        for dc in range(2):
            for dy in range(NY):
                g_copy(dy, dc).start()

    def finish(s):
        wait_bytes(zin.at[s, 7], z_recv.at[s, 7])
        wait_bytes(zin.at[s, 8], z_recv.at[s, 8])
        wide[pl.ds(LAST, WIN)] = part[s, 7] + zin[s, 7] + zin[s, 8]
        kinds = columns_irrep(7)
        begins = [LAST - window(3 * core + s, kind) for kind in range(NIRREP)]
        for block in range(NY):

            def unpack(row):
                rows = wide[begins[0] + block * (BLK // SUB) + row]
                for kind in range(1, NIRREP):
                    rows = jnp.where(kinds == kind, wide[begins[kind] + block * (BLK // SUB) + row], rows)
                for half in range(2):
                    yout[s, 2 * block + half, row] = rows[:, half * BLK:(half + 1) * BLK]

            loop(BLK // SUB, unpack, unroll=True)
        for dc in range(2):
            for dy in range(NY):
                y_copy(s, dy, dc).start()

    def mask(i, total):
        rows = irrep(BLK * gx + lax.broadcasted_iota(jnp.int32, (BLK, 1), 0))
        columns = irrep(BLK * gy + lax.broadcasted_iota(jnp.int32, (1, BLK), 1))
        return jnp.where((rows ^ columns) == pair_irrep(i), total, 0.0)

    def write_gathered(g):
        i = NS * g + NS - 1
        wait_bytes(gin.at[pl.ds(NY * g, NY)], g_recv.at[g])
        for block in range(NY):
            narrow[pl.ds(LAST + SHARE * block, QUARTER)] = gin[NY * g + block]
        kinds = irrep(BLK * gy + lax.broadcasted_iota(jnp.int32, (1, BLK), 1))
        begins = [LAST - window(i, kind) + y * (BLK // SUB) for kind in range(NIRREP)]

        def unpack(row):
            rows = narrow[begins[0] + row]
            for kind in range(1, NIRREP):
                rows = jnp.where(kinds == kind, narrow[begins[kind] + row], rows)
            flat[row] = rows

        loop(BLK // SUB, unpack, unroll=True)
        out[i] = mask(i, 2.0 * flat[...].reshape(BLK, BLK))

    def write(i):
        wait_bytes(yin.at[i], y_recv.at[i])
        total = 2.0 * (yin[i, 0] + yin[i, 1] + yin[i, 2] + yin[i, 3]).reshape(BLK, BLK)
        out[i] = mask(i, total)

    actions = dict(
        amp=send_amplitudes, own=send_integrals, got=take_amplitudes, share=take_integrals, have=take_shared,
        quarter=pass_quarter, finish=finish,
    )

    def look_up(n, values):
        found = jnp.int32(values[0])
        for place, value in enumerate(values[1:], 1):
            found = jnp.where(n == place, value, found)
        return found

    def act(names):
        for name, arg in names:
            actions[name](arg)

    for ref, size in ((wide, TILE), (narrow, BLK)):
        ref[pl.ds(0, LAST)] = jnp.zeros((LAST, SUB, size), F32)
        ref[pl.ds(ROWS, LAST)] = jnp.zeros((LAST, SUB, size), F32)
    act(BEFORE)

    def one(n):
        for place in range(len(UNITS)):
            if EARLY[place]:

                @pl.when(n == place)
                def _():
                    act(EARLY[place])

        s, step = look_up(n, [s for s, _ in UNITS]), look_up(n, [step for _, step in UNITS])
        compute(s, step)

        @pl.when(s == NS - 1)
        def _():
            split_rows(step)

        @pl.when(s < NS - 1)
        def _():
            pass_on(s, step)

    loop(len(UNITS), one)
    act(AFTER)
    loop(4, lambda n: write(3 * lax.rem(n, 2) + lax.div(n, 2)))
    loop(2, write_gathered)

    def drain(s):
        wait_bytes(left.at[s, pl.ds(0, 448), :], t_send.at[s])

        @pl.when(s < NS - 1)
        def _():
            for copy in z_first(s):
                copy.wait_send()
            loop(6, lambda step: z_copy(s, step + 1).wait_send())
            wait_bytes(yout.at[s, pl.ds(0, 7)], y_send.at[s])

    loop(NS, drain)

    def drain_step(step):
        wait_bytes(right.at[step, 0, :, pl.ds(0, 3)], w_send.at[step])
        share_integrals(step).wait_send()
        wait_bytes(split.at[step, pl.ds(0, NY - 1)], s_send.at[step])

    loop(NZ, drain_step)
    for copy in q_first():
        copy.wait_send()
    loop(6, lambda step: q_copy(step + 1).wait_send())
    wait_bytes(gin.at[pl.ds(0, 7)], g_send)


def per_device(amplitudes, coulomb, exchange_ints, block_sizes, occ_irreps, tile_i, tile_j):
    depth, columns = coulomb.shape[1], coulomb.shape[3]
    count = amplitudes.shape[0]
    anywhere, scalars = pl.BlockSpec(memory_space=pl.ANY), pl.BlockSpec(memory_space=pltpu.SMEM)
    dma = pltpu.SemaphoreType.DMA
    residual = pl.pallas_call(
        kernel,
        out_shape=jax.ShapeDtypeStruct((count, BLK, BLK), F32),
        in_specs=[anywhere] * 3 + [scalars] * 4,
        out_specs=pl.BlockSpec(memory_space=pltpu.VMEM),
        scratch_shapes=[
            pltpu.VMEM((NS, GRP, 4 * GRP), jnp.bfloat16),
            pltpu.VMEM((NS, 2, GRP, GRP), jnp.bfloat16),
            pltpu.VMEM((NZ, 2, 2, NX, BLK, TILE), jnp.bfloat16),
            pltpu.VMEM((ROWS, SUB, TILE), F32),
            pltpu.VMEM((NS, NZ, WIN, SUB, TILE), F32),
            pltpu.VMEM((NS - 1, NZ + 1, WIN, SUB, TILE), F32),
            pltpu.VMEM((ROWS + LAST, SUB, TILE), F32),
            pltpu.VMEM((NS - 1, 2 * NY, BLK // SUB, SUB, BLK), F32),
            pltpu.VMEM((2 * NS, NY, BLK // SUB, SUB, BLK), F32),
            pltpu.VMEM((NZ, NY, QUARTER, SUB, TILE), F32),
            pltpu.VMEM((NZ, QUARTER, SUB, TILE), F32),
            pltpu.VMEM((NZ + 1, QUARTER, SUB, TILE), F32),
            pltpu.VMEM((2, QUARTER, SUB, BLK), F32),
            pltpu.VMEM((2 * NY, QUARTER, SUB, BLK), F32),
            pltpu.VMEM((ROWS + LAST, SUB, BLK), F32),
            pltpu.VMEM((BLK // SUB, SUB, BLK), F32),
            dma((NS,)), dma((NS,)), dma((NS,)),
            dma((NZ,)), dma((NZ,)), dma((NZ,)), dma((NZ,)),
            dma((NS, NZ + 1)), dma((NS, NZ)),
            dma((2 * NS,)), dma((NS,)),
            dma((NZ,)), dma((NZ,)), dma((NZ + 1,)), dma((NZ,)),
            dma((2,)), dma,
        ],
        compiler_params=pltpu.CompilerParams(
            collective_id=0, has_side_effects=True, vmem_limit_bytes=56 * 1024 * 1024
        ),
        cost_estimate=pl.CostEstimate(flops=12900000000, bytes_accessed=5000000, transcendentals=0),
    )(
        amplitudes.reshape(count, BLK, columns),
        coulomb.reshape(depth, columns),
        exchange_ints.reshape(depth, columns),
        block_sizes, occ_irreps, tile_i, tile_j,
    )
    return residual.reshape(count, BLK, 1, BLK)


def solution(mesh):
    return jax.shard_map(
        per_device,
        mesh=mesh,
        in_specs=(
            P(None, "gy", "gx", None),
            P("gy", "gx", None, None),
            P("gy", "gx", None, None),
            P(),
            P(),
            P(),
            P(),
        ),
        out_specs=P(None, "gx", None, "gy"),
        check_vma=False,
    )
```

```python
import jax
import jax.numpy as jnp
from jax import lax
from jax.experimental import pallas as pl
from jax.experimental.pallas import tpu as pltpu
from jax.sharding import PartitionSpec as P

MESH = pl.DeviceIdType.MESH
NY, NX, NZ = 4, 4, 8
NIRREP = 4
NS = 3
BLK = 128
GRP = NY * BLK
TILE = 256
SUB = 8
ROWS = GRP // SUB
WIN = 33
LAST = ROWS - WIN
SHARE, QUARTER = 8, 9
UPPER, LOWER = pl.ds(0, 17), pl.ds(17, 16)
Q_UPPER, Q_LOWER = pl.ds(0, 5), pl.ds(5, 4)
F32 = jnp.float32


def make_plan():
    units = sorted(
        [(s, step) for s in range(NS) for step in range(NZ)], key=lambda unit: ((unit[1] + 1) // 2, unit[0], unit[1])
    )
    before = [("amp", s) for s in range(NS)] + [("own", step) for step in range(NZ)]
    early = [[] for _ in units]
    for s in range(NS):
        early[units.index((s, 0))] += [("got", s)]
    for step in range(NZ):
        early[units.index((0, step))] += [("share", step), ("have", step)]
    after = [("finish", 0), ("finish", 1)]
    for step in range(NZ):
        place = units.index((NS - 1, step)) + 7
        (early[place] if place < len(units) else after).append(("quarter", step))
    return units, before, early, after


UNITS, BEFORE, EARLY, AFTER = make_plan()


def step_tile(step):
    half = lax.div(step + 1, 2)
    return 4 + half * (1 - 2 * lax.rem(step, 2))


def kernel(amp, coul, exch, sizes, occ, tile_i, tile_j, out, left, raw, right, dense, part, zin, wide, yout, yin,
           split, quarter, qin, gout, gin, narrow, flat,
           t1_recv, t2_recv, t_send, w_recv, w_send, c_recv, c_send, z_recv, z_send, y_recv, y_send,
           s_recv, s_send, q_recv, q_send, g_recv, g_send):
    gx, gy = lax.axis_index("gx"), lax.axis_index("gy")
    y, x = lax.div(gx, NX), lax.rem(gx, NX)
    z, core = lax.div(gy, 2), lax.rem(gy, 2)

    def device(dy=0, dx=0, dz=0, dc=0):
        y2, x2 = lax.rem(y + dy, NY), lax.rem(x + dx, NX)
        z2, core2 = lax.rem(z + dz, NZ), lax.rem(core + dc, 2)
        return (y2 * NX + x2, z2 * 2 + core2)

    barrier = pltpu.get_barrier_semaphore()
    partners = [dict(dy=dy, dc=dc) for dy in range(NY) for dc in range(2) if dy or dc]
    partners += [dict(dx=dx, dc=dc) for dx in range(1, NX) for dc in range(2)]
    partners += [dict(dz=1), dict(dz=NZ - 1)]
    for partner in partners:
        pl.semaphore_signal(barrier, inc=1, device_id=device(**partner), device_id_type=MESH)
    pl.semaphore_wait(barrier, len(partners))

    def loop(count, body, unroll=None):
        lax.fori_loop(0, count, lambda n, carry: (body(n), carry)[1], 0, unroll=unroll)

    def send_amplitudes(s):
        for dc in range(2):
            row = 3 * lax.rem(core + dc, 2) + s
            for dy in range(NY):
                y2 = lax.rem(y + dy, NY)
                src = amp.at[row, :, pl.ds(pl.multiple_of(GRP * y2, GRP), GRP)]
                dst = left.at[s, pl.ds(pl.multiple_of(BLK * y, BLK), BLK), pl.ds(pl.multiple_of(GRP * core, GRP), GRP)]
                if dy or dc:
                    pltpu.make_async_remote_copy(
                        src, dst, t_send.at[s], t1_recv.at[s], device_id=device(dy=dy, dc=dc), device_id_type=MESH
                    ).start()
                else:
                    pltpu.make_async_copy(src, dst, t1_recv.at[s]).start()
            for dx in range(NX):
                x2 = lax.rem(x + dx, NX)
                for y2 in range(NY):
                    src = amp.at[row, :, pl.ds(pl.multiple_of(GRP * y2 + BLK * x2, BLK), BLK)]
                    dst = raw.at[s, core, pl.ds(pl.multiple_of(BLK * x, BLK), BLK), pl.ds(BLK * y2, BLK)]
                    if dx or dc:
                        pltpu.make_async_remote_copy(
                            src, dst, t_send.at[s], t2_recv.at[s], device_id=device(dx=dx, dc=dc), device_id_type=MESH
                        ).start()
                    else:
                        pltpu.make_async_copy(src, dst, t2_recv.at[s]).start()

    def send_integrals(step):
        tile = lax.rem(z + step_tile(step), NZ)
        columns = pl.ds(pl.multiple_of(TILE * tile, TILE), TILE)
        for dx in (1, 3, 2, 0):
            for term, ref in ((0, coul), (1, exch)):
                src, dst = ref.at[:, columns], right.at[step, term, core, x]
                if dx:
                    pltpu.make_async_remote_copy(
                        src, dst, w_send.at[step], w_recv.at[step], device_id=device(dx=dx), device_id_type=MESH
                    ).start()
                else:
                    pltpu.make_async_copy(src, dst, w_recv.at[step]).start()

    def wait_bytes(ref, sem):
        pltpu.make_async_copy(ref, ref, sem).wait()

    def take_amplitudes(s):
        wait_bytes(left.at[s, :, pl.ds(0, 2 * GRP)], t1_recv.at[s])
        wait_bytes(raw.at[s], t2_recv.at[s])
        for k in range(2):
            left[s, :, pl.ds((2 + k) * GRP, GRP)] = (raw[s, k] * jnp.asarray(-0.5, jnp.bfloat16)).T

    def share_integrals(step):
        return pltpu.make_async_remote_copy(
            right.at[step, :, core], right.at[step, :, core], c_send.at[step], c_recv.at[step],
            device_id=device(dc=1), device_id_type=MESH,
        )

    def take_integrals(step):
        wait_bytes(right.at[step, :, core], w_recv.at[step])
        share_integrals(step).start()

    def take_shared(step):
        wait_bytes(right.at[step, :, 1 - core], c_recv.at[step])

    first_end = sizes[0]
    second_end = first_end + sizes[1]
    third_end = second_end + sizes[2]

    def irrep(index):
        return (
            (index >= first_end).astype(jnp.int32)
            + (index >= second_end).astype(jnp.int32)
            + (index >= third_end).astype(jnp.int32)
        )

    def pair_irrep(i):
        return occ[tile_i[i]] ^ occ[tile_j[0]]

    def window(i, col_irrep):
        row_irrep = pair_irrep(i) ^ col_irrep
        begin = jnp.where(row_irrep > 0, sizes[0], 0) + jnp.where(row_irrep > 1, sizes[1], 0)
        begin = begin + jnp.where(row_irrep > 2, sizes[2], 0)
        block = lax.div(begin, GRP)
        local = block * BLK + jnp.clip(begin - block * GRP - BLK * x, 0, BLK)
        return jnp.minimum(lax.div(local, SUB), LAST)

    def columns_irrep(step):
        tile = lax.rem(z + step_tile(step), NZ)
        return irrep(TILE * tile + lax.broadcasted_iota(jnp.int32, (1, TILE), 1))

    def z_copy(s, step):
        up = lax.rem(step, 2)
        return pltpu.make_async_remote_copy(
            part.at[s, step], zin.at[s, step + 2], z_send.at[s, step], z_recv.at[s, step + 2],
            device_id=device(dz=up + (1 - up) * (NZ - 1)), device_id_type=MESH,
        )

    def z_first(s):
        return [
            pltpu.make_async_remote_copy(
                part.at[s, 0, rows], zin.at[s, slot, rows], z_send.at[s, sem], z_recv.at[s, slot],
                device_id=device(dz=dz), device_id_type=MESH,
            )
            for rows, slot, sem, dz in ((UPPER, 1, 0, 1), (LOWER, 2, 7, NZ - 1))
        ]

    def q_copy(step):
        up = lax.rem(step, 2)
        return pltpu.make_async_remote_copy(
            quarter.at[step], qin.at[step + 2], q_send.at[step], q_recv.at[step + 2],
            device_id=device(dz=up + (1 - up) * (NZ - 1)), device_id_type=MESH,
        )

    def q_first():
        return [
            pltpu.make_async_remote_copy(
                quarter.at[0, rows], qin.at[slot, rows], q_send.at[sem], q_recv.at[slot],
                device_id=device(dz=dz), device_id_type=MESH,
            )
            for rows, slot, sem, dz in ((Q_UPPER, 1, 0, 1), (Q_LOWER, 2, 7, NZ - 1))
        ]

    def split_rows(step):
        for dy in (2, 1, 3):
            y2 = lax.rem(y + dy, NY)
            pltpu.make_async_remote_copy(
                part.at[NS - 1, step, pl.ds(SHARE * y2, QUARTER)], split.at[step, y], s_send.at[step], s_recv.at[step],
                device_id=device(dy=dy), device_id_type=MESH,
            ).start()

    def g_copy(dy, dc):
        core2 = lax.rem(core + dc, 2)
        src, dst = gout.at[core2], gin.at[NY * core + y]
        if dy or dc:
            return pltpu.make_async_remote_copy(
                src, dst, g_send, g_recv.at[core], device_id=device(dy=dy, dc=dc), device_id_type=MESH
            )
        return pltpu.make_async_copy(src, dst, g_recv.at[core])

    def y_copy(s, dy, dc):
        y2, core2 = lax.rem(y + dy, NY), lax.rem(core + dc, 2)
        src, dst = yout.at[s, 2 * y2 + core2], yin.at[3 * core + s, y]
        if dy or dc:
            return pltpu.make_async_remote_copy(
                src, dst, y_send.at[s], y_recv.at[3 * core + s], device_id=device(dy=dy, dc=dc), device_id_type=MESH
            )
        return pltpu.make_async_copy(src, dst, y_recv.at[3 * core + s])

    def compute(s, step):
        product = jnp.dot(left[s], right[step].reshape(4 * GRP, TILE), preferred_element_type=F32)
        dense[...] = product.reshape(ROWS, SUB, TILE)
        kinds = columns_irrep(step)
        begins = [window(3 * core + s, kind) for kind in range(NIRREP)]

        def pack(row):
            packed = dense[begins[0] + row]
            for kind in range(1, NIRREP):
                packed = jnp.where(kinds == kind, dense[begins[kind] + row], packed)
            part[s, step, row] = packed

        loop(WIN, pack, unroll=True)

    def pass_on(s, step):
        @pl.when(step == 0)
        def _():
            for copy in z_first(s):
                copy.start()

        for place, rows in ((1, UPPER), (2, LOWER)):

            @pl.when(step == place)
            def _():
                wait_bytes(zin.at[s, place, rows], z_recv.at[s, place])
                part[s, place, rows] += zin[s, place, rows]

        @pl.when((step > 2) & (step < 7))
        def _():
            wait_bytes(zin.at[s, step], z_recv.at[s, step])
            part[s, step] += zin[s, step]

        @pl.when((step > 0) & (step < 7))
        def _():
            z_copy(s, step).start()

    def pass_quarter(step):
        wait_bytes(split.at[step, pl.ds(0, NY - 1)], s_recv.at[step])
        total = part[NS - 1, step, pl.ds(SHARE * y, QUARTER)]
        for dy in range(1, NY):
            total = total + split[step, lax.rem(y + dy, NY)]
        quarter[step] = total
        if step == 0:
            for copy in q_first():
                copy.start()
            return
        for slot in (7, 8) if step == 7 else (step,):
            rows = {1: Q_UPPER, 2: Q_LOWER}.get(slot, pl.ds(0, QUARTER))
            wait_bytes(qin.at[slot, rows], q_recv.at[slot])
            quarter[step, rows] += qin[slot, rows]
        if step < 7:
            q_copy(step).start()
            return
        for half in range(2):
            gout[half] = quarter[7, :, :, pl.ds(half * BLK, BLK)]
        for dc in range(2):
            for dy in (2, 1, 3, 0):
                g_copy(dy, dc).start()

    def finish(s):
        wait_bytes(zin.at[s, 7], z_recv.at[s, 7])
        wait_bytes(zin.at[s, 8], z_recv.at[s, 8])
        wide[pl.ds(LAST, WIN)] = part[s, 7] + zin[s, 7] + zin[s, 8]
        kinds = columns_irrep(7)
        begins = [LAST - window(3 * core + s, kind) for kind in range(NIRREP)]
        for block in range(NY):

            def unpack(row):
                rows = wide[begins[0] + block * (BLK // SUB) + row]
                for kind in range(1, NIRREP):
                    rows = jnp.where(kinds == kind, wide[begins[kind] + block * (BLK // SUB) + row], rows)
                for half in range(2):
                    yout[s, 2 * block + half, row] = rows[:, half * BLK:(half + 1) * BLK]

            loop(BLK // SUB, unpack, unroll=True)
        for dc in range(2):
            for dy in (2, 1, 3, 0):
                y_copy(s, dy, dc).start()

    def mask(i, total):
        rows = irrep(BLK * gx + lax.broadcasted_iota(jnp.int32, (BLK, 1), 0))
        columns = irrep(BLK * gy + lax.broadcasted_iota(jnp.int32, (1, BLK), 1))
        return jnp.where((rows ^ columns) == pair_irrep(i), total, 0.0)

    def write_gathered(g):
        i = NS * g + NS - 1
        wait_bytes(gin.at[pl.ds(NY * g, NY)], g_recv.at[g])
        for block in range(NY):
            narrow[pl.ds(LAST + SHARE * block, QUARTER)] = gin[NY * g + block]
        kinds = irrep(BLK * gy + lax.broadcasted_iota(jnp.int32, (1, BLK), 1))
        begins = [LAST - window(i, kind) + y * (BLK // SUB) for kind in range(NIRREP)]

        def unpack(row):
            rows = narrow[begins[0] + row]
            for kind in range(1, NIRREP):
                rows = jnp.where(kinds == kind, narrow[begins[kind] + row], rows)
            flat[row] = rows

        loop(BLK // SUB, unpack, unroll=True)
        out[i] = mask(i, 2.0 * flat[...].reshape(BLK, BLK))

    def write(i):
        wait_bytes(yin.at[i], y_recv.at[i])
        total = 2.0 * (yin[i, 0] + yin[i, 1] + yin[i, 2] + yin[i, 3]).reshape(BLK, BLK)
        out[i] = mask(i, total)

    actions = dict(
        amp=send_amplitudes, own=send_integrals, got=take_amplitudes, share=take_integrals, have=take_shared,
        quarter=pass_quarter, finish=finish,
    )

    def look_up(n, values):
        found = jnp.int32(values[0])
        for place, value in enumerate(values[1:], 1):
            found = jnp.where(n == place, value, found)
        return found

    def act(names):
        for name, arg in names:
            actions[name](arg)

    act(BEFORE)
    for ref, size in ((wide, TILE), (narrow, BLK)):
        ref[pl.ds(0, LAST)] = jnp.zeros((LAST, SUB, size), F32)
        ref[pl.ds(ROWS, LAST)] = jnp.zeros((LAST, SUB, size), F32)

    def one(n):
        for place in range(len(UNITS)):
            if EARLY[place]:

                @pl.when(n == place)
                def _():
                    act(EARLY[place])

        s, step = look_up(n, [s for s, _ in UNITS]), look_up(n, [step for _, step in UNITS])
        compute(s, step)

        @pl.when(s == NS - 1)
        def _():
            split_rows(step)

        @pl.when(s < NS - 1)
        def _():
            pass_on(s, step)

    loop(len(UNITS), one)
    act(AFTER)
    loop(4, lambda n: write(3 * lax.rem(n, 2) + lax.div(n, 2)))
    loop(2, write_gathered)

    def drain(s):
        wait_bytes(left.at[s, pl.ds(0, 448), :], t_send.at[s])

        @pl.when(s < NS - 1)
        def _():
            for copy in z_first(s):
                copy.wait_send()
            loop(6, lambda step: z_copy(s, step + 1).wait_send())
            wait_bytes(yout.at[s, pl.ds(0, 7)], y_send.at[s])

    loop(NS, drain)

    def drain_step(step):
        wait_bytes(right.at[step, 0, :, pl.ds(0, 3)], w_send.at[step])
        share_integrals(step).wait_send()
        wait_bytes(split.at[step, pl.ds(0, NY - 1)], s_send.at[step])

    loop(NZ, drain_step)
    for copy in q_first():
        copy.wait_send()
    loop(6, lambda step: q_copy(step + 1).wait_send())
    wait_bytes(gin.at[pl.ds(0, 7)], g_send)


def per_device(amplitudes, coulomb, exchange_ints, block_sizes, occ_irreps, tile_i, tile_j):
    depth, columns = coulomb.shape[1], coulomb.shape[3]
    count = amplitudes.shape[0]
    anywhere, scalars = pl.BlockSpec(memory_space=pl.ANY), pl.BlockSpec(memory_space=pltpu.SMEM)
    dma = pltpu.SemaphoreType.DMA
    residual = pl.pallas_call(
        kernel,
        out_shape=jax.ShapeDtypeStruct((count, BLK, BLK), F32),
        in_specs=[anywhere] * 3 + [scalars] * 4,
        out_specs=pl.BlockSpec(memory_space=pltpu.VMEM),
        scratch_shapes=[
            pltpu.VMEM((NS, GRP, 4 * GRP), jnp.bfloat16),
            pltpu.VMEM((NS, 2, GRP, GRP), jnp.bfloat16),
            pltpu.VMEM((NZ, 2, 2, NX, BLK, TILE), jnp.bfloat16),
            pltpu.VMEM((ROWS, SUB, TILE), F32),
            pltpu.VMEM((NS, NZ, WIN, SUB, TILE), F32),
            pltpu.VMEM((NS - 1, NZ + 1, WIN, SUB, TILE), F32),
            pltpu.VMEM((ROWS + LAST, SUB, TILE), F32),
            pltpu.VMEM((NS - 1, 2 * NY, BLK // SUB, SUB, BLK), F32),
            pltpu.VMEM((2 * NS, NY, BLK // SUB, SUB, BLK), F32),
            pltpu.VMEM((NZ, NY, QUARTER, SUB, TILE), F32),
            pltpu.VMEM((NZ, QUARTER, SUB, TILE), F32),
            pltpu.VMEM((NZ + 1, QUARTER, SUB, TILE), F32),
            pltpu.VMEM((2, QUARTER, SUB, BLK), F32),
            pltpu.VMEM((2 * NY, QUARTER, SUB, BLK), F32),
            pltpu.VMEM((ROWS + LAST, SUB, BLK), F32),
            pltpu.VMEM((BLK // SUB, SUB, BLK), F32),
            dma((NS,)), dma((NS,)), dma((NS,)),
            dma((NZ,)), dma((NZ,)), dma((NZ,)), dma((NZ,)),
            dma((NS, NZ + 1)), dma((NS, NZ)),
            dma((2 * NS,)), dma((NS,)),
            dma((NZ,)), dma((NZ,)), dma((NZ + 1,)), dma((NZ,)),
            dma((2,)), dma,
        ],
        compiler_params=pltpu.CompilerParams(
            collective_id=0, has_side_effects=True, vmem_limit_bytes=56 * 1024 * 1024
        ),
        cost_estimate=pl.CostEstimate(flops=12900000000, bytes_accessed=5000000, transcendentals=0),
    )(
        amplitudes.reshape(count, BLK, columns),
        coulomb.reshape(depth, columns),
        exchange_ints.reshape(depth, columns),
        block_sizes, occ_irreps, tile_i, tile_j,
    )
    return residual.reshape(count, BLK, 1, BLK)


def solution(mesh):
    return jax.shard_map(
        per_device,
        mesh=mesh,
        in_specs=(
            P(None, "gy", "gx", None),
            P("gy", "gx", None, None),
            P("gy", "gx", None, None),
            P(),
            P(),
            P(),
            P(),
        ),
        out_specs=P(None, "gx", None, "gy"),
        check_vma=False,
    )
```
